512 devices in a mesh: freq: 8 (over y, core), tm: 64 (over z, x).
Axes of the slice: x: 4, y: 4, z: 16, core: 2. Of those that a mesh axis runs over, the one named last changes fastest.
Arguments:
- audio: bfloat16 [64, 8388608], P('tm', 'freq'), may hold values from -8 to 8
- w_start: float32 [32, 4096], P(None, 'freq'), may hold values from 0.05 to 0.5
- h_start: float32 [32, 65536], P(None, 'tm'), may hold values from 0.05 to 0.5
Outputs:
- components: float32 [32, 4096], P(None, 'freq')
- activations: float32 [32, 65536], P(None, 'tm')
The draws below stay inside these ranges and needn't reach their ends.
All inputs are finite; a program needn't handle non-finite values.
Results may differ from the reference program's by a relative error of at most 0.00053.
Values may be sent and summed in bfloat16 or wider, within the bound.
A program may use at most 64 MiB of HBM per device.

```python
import math
import jax
import jax.numpy as jnp
from jax import lax

BINS = 4096
COMP = 32
FR_SUB = 128
ITERS = 2
FRAMES = 65536
N_FREQ = 8
N_TM = 64


def upsample(values, factor):
    spread = jnp.broadcast_to(values[..., None], values.shape + (factor,))
    return spread.reshape(values.shape[:-1] + (values.shape[-1] * factor,))


def log_uniform(key, shape_given, low_value, high_value):
    return jnp.exp(jax.random.uniform(key, shape_given, minval=math.log(low_value), maxval=math.log(high_value)))


def draw_audio(key, part):
    key = jax.random.fold_in(key, 7)
    row_count = N_TM
    frame_count = N_FREQ * FR_SUB
    frame_len = 2 * BINS
    tone_count = 16
    band_count = 8
    subkeys = jax.random.split(key, 15)
    full_shape = (row_count, frame_count, frame_len)
    position = jnp.arange(frame_len, dtype=jnp.int32)
    tone_bins = jax.random.randint(subkeys[0], (tone_count,), 4, BINS - 4)
    band_bins = jax.random.randint(subkeys[1], (band_count,), 16, BINS - 16)
    tone_base = log_uniform(subkeys[2], (tone_count,), 0.3, 3.0)
    band_base = log_uniform(subkeys[3], (band_count,), 0.05, 0.4)
    tone_phase = jax.random.uniform(subkeys[4], (row_count, frame_count, tone_count), minval=-math.pi, maxval=math.pi)
    tone_swing = jnp.exp(0.6 * jax.random.normal(subkeys[5], (row_count, frame_count, tone_count)))
    tone_onset = 0.15 + jax.random.bernoulli(subkeys[6], 0.6, (row_count, frame_count, tone_count)).astype(jnp.float32)
    band_swing = jnp.exp(0.6 * jax.random.normal(subkeys[7], (row_count, frame_count, band_count)))
    band_onset = 0.15 + jax.random.bernoulli(subkeys[8], 0.6, (row_count, frame_count, band_count)).astype(jnp.float32)
    frame_gain = log_uniform(subkeys[9], (row_count, frame_count, 1), 0.5, 2.0)
    coarse_noise = upsample(jax.random.normal(subkeys[10], (row_count, frame_count, frame_len // 16)), 16)
    slow_noise = upsample(jax.random.normal(subkeys[11], (row_count, frame_count, frame_len // 128)), 128)
    white_noise = jax.random.normal(subkeys[12], full_shape)
    signal = frame_gain * (0.25 * white_noise + 0.5 * coarse_noise + 0.25 * slow_noise)
    tone_scale = 8.0 / math.sqrt(frame_len)
    for source in range(tone_count):
        turns = (tone_bins[source] * position % frame_len).astype(jnp.float32)
        phase_angle = 2.0 * math.pi * turns / frame_len + tone_phase[:, :, source:source + 1]
        level = tone_scale * tone_base[source] * tone_swing[:, :, source:source + 1] * tone_onset[:, :, source:source + 1]
        signal = signal + level * jnp.cos(phase_angle)
    band_noise = jax.random.normal(subkeys[14], (band_count, row_count, frame_count, frame_len // 256))
    for source in range(band_count):
        envelope = upsample(band_noise[source], 256)
        turns = (band_bins[source] * position % frame_len).astype(jnp.float32)
        phase_angle = 2.0 * math.pi * turns / frame_len
        level = band_base[source] * band_swing[:, :, source:source + 1] * band_onset[:, :, source:source + 1]
        signal = signal + level * envelope * jnp.cos(phase_angle)
    signal = jnp.clip(signal, -8.0, 8.0)
    return signal.reshape(row_count, frame_count * frame_len).astype(jnp.bfloat16)


def block_levels(stream_key, extent, cuts, least, largest):
    loudness, own = 1.0, jax.random.fold_in(stream_key, 6)
    for dim, shards_of in cuts:
        steps = jnp.exp(jax.random.uniform(jax.random.fold_in(own, dim), (shards_of,), jnp.float32, least / len(cuts), largest / len(cuts)))
        loudness = loudness * jnp.repeat(steps, extent[dim] // shards_of).reshape([-1 if axis == dim else 1 for axis in range(len(extent))])
    return loudness


def setup_inputs(seed: int = 0) -> dict:
    keys = jax.random.split(jax.random.key(seed), 4)
    return {
        "audio": draw_audio(jax.random.fold_in(keys[3], 71), 0),
        "w_start": jnp.clip(jnp.exp(math.log(0.5) - 2.3025851 * jax.random.uniform(keys[1], (COMP, BINS), jnp.float32) ** block_levels(keys[1], (COMP, BINS), ((1, 8),), -0.2, 0.2)), 0.05, 0.5),
        "h_start": jnp.clip(jnp.exp(math.log(0.5) - 2.3025851 * jax.random.uniform(keys[2], (COMP, FRAMES), jnp.float32) ** block_levels(keys[2], (COMP, FRAMES), ((1, 64),), -0.2, 0.2)), 0.05, 0.5),
    }


def reference(audio, w_start, h_start):
    frame_len = 2 * BINS
    signal = audio.reshape(-1, FR_SUB, frame_len)
    position = jnp.arange(frame_len).astype(jnp.float32)
    window = 0.5 - 0.5 * jnp.cos(2.0 * math.pi * position / frame_len)
    factor = 1.0 / math.sqrt(0.375 * frame_len)

    def one_block(block):
        windowed = block.astype(jnp.float32) * window
        transform = jnp.fft.rfft(windowed, axis=-1)[:, :BINS]
        real_part = jnp.real(transform)
        imag_part = jnp.imag(transform)
        return (jnp.sqrt(real_part * real_part + imag_part * imag_part) * factor).astype(jnp.bfloat16)
    magnitude = lax.map(one_block, signal).reshape(-1, BINS)
    highest = lax.Precision.HIGHEST
    components = w_start
    activations = h_start
    for step in range(ITERS):
        numer_h = jnp.dot(components.astype(jnp.bfloat16), magnitude.T, preferred_element_type=jnp.float32)
        gram_w = jnp.dot(components, components.T, precision=highest)
        activations = activations * numer_h / jnp.dot(gram_w, activations, precision=highest)
        numer_w = jnp.dot(activations.astype(jnp.bfloat16), magnitude, preferred_element_type=jnp.float32)
        gram_h = jnp.dot(activations, activations.T, precision=highest)
        components = components * numer_w / jnp.dot(gram_h, components, precision=highest)
    return (components, activations)
```

```python
import functools
import math

import jax
import jax.numpy as jnp
import ml_dtypes
import numpy as np
from jax import lax
from jax.experimental import pallas as pl
from jax.experimental.pallas import tpu as pltpu
from jax.sharding import PartitionSpec as P

MESH = pl.DeviceIdType.MESH
HIGHEST = lax.Precision.HIGHEST
F32 = jnp.float32
B16 = jnp.bfloat16

BINS = 4096
FRAME = 2 * BINS
ITERS = 2
COMP = 32
OUTER = 64
INNER = 128
NX, NY, NZ, NC = 4, 4, 16, 2
NF = NY * NC
NQ = NX * NY
OWN = BINS // NF
FRAMES = 128
GROUP = 16
GROUPS = FRAMES // GROUP
HALF_K = OUTER // 2
NK = HALF_K + 2
ROWS = COMP + 8
WROWS = COMP + 16


def two_terms(values):
    hi = values.astype(np.float32).astype(ml_dtypes.bfloat16)
    lo = (values - hi.astype(np.float64)).astype(np.float32).astype(ml_dtypes.bfloat16)
    return hi, lo


def tables():
    outer, inner, k = np.arange(OUTER), np.arange(INNER), np.arange(NK)
    angle = 2 * np.pi * (np.outer(k, outer) % OUTER) / OUTER
    first = np.zeros((2, NK, 8, 8, OUTER))
    for frame in range(8):
        first[0, :, frame, frame] = np.cos(angle)
        first[1, :, frame, frame] = -np.sin(angle)
    first_hi, first_lo = two_terms(first.reshape(2 * NK * 8, 8 * OUTER))
    angle = 2 * np.pi * np.outer(k, inner) / FRAME
    scale = 0.5 / math.sqrt(0.375 * FRAME)
    twist = np.stack([np.cos(angle) * scale, np.sin(angle) * scale])
    twist = np.concatenate([twist, twist], -1)[:, :, None, :]
    twist = np.ascontiguousarray(np.broadcast_to(twist, (2, NK, 8, 2 * INNER))).astype(np.float32)
    row = np.arange(INNER)
    second_k = np.where(row < 64, row, 191 - row)
    angle = 2 * np.pi * (np.outer(second_k, inner) % INNER) / INNER
    second_hi, second_lo = two_terms(
        np.block([[np.cos(angle), np.sin(angle)], [-np.sin(angle), np.cos(angle)]])
    )
    place = np.zeros((OWN, OWN), np.float32)
    for k1 in range(OUTER):
        at = k1 if k1 <= HALF_K else 3 * HALF_K - k1
        for k2 in range(8):
            place[OUTER * k2 + k1, at * 8 + k2] = 1.0
    return first_hi, first_lo, twist, second_hi, second_lo, place.astype(ml_dtypes.bfloat16)


def dot(a, b, precision=None):
    dims = (((1,), (0,)), ((), ()))
    return lax.dot_general(a, b, dims, precision=precision, preferred_element_type=F32)


def dot_t(a, b, precision=None):
    dims = (((1,), (1,)), ((), ()))
    return lax.dot_general(a, b, dims, precision=precision, preferred_element_type=F32)


def terms(value):
    hi = value.astype(B16)
    rest = value - hi.astype(F32)
    mid = rest.astype(B16)
    return hi, mid, (rest - mid.astype(F32)).astype(B16)


def pack(gram):
    return jnp.concatenate([gram[8 * i : 8 * i + 8] for i in range(4)], axis=1)


def unpack(tile):
    return jnp.concatenate([tile[:, 32 * i : 32 * i + 32] for i in range(4)], axis=0)


def gather_slot(block):
    tile = pack(dot_t(block, block, HIGHEST))
    hi = tile.astype(B16)
    lo = (tile - hi.astype(F32)).astype(B16)
    return jnp.concatenate([block.astype(B16), hi, lo], axis=0)


def first_stage(audio, first_hi, first_lo, twist, outer, g_hi, g_lo, g):
    span = 8 * FRAME
    start = pl.multiple_of(g * (2 * span), 2 * span)
    left = audio[:, pl.ds(start, span)].reshape(8 * OUTER, INNER)
    right = audio[:, pl.ds(start + span, span)].reshape(8 * OUTER, INNER)
    both = jnp.concatenate([left, right], axis=1)
    outer[...] = (dot(first_hi[...], both) + dot(first_lo[...], both)).reshape(outer.shape)
    frame = pl.multiple_of(g * GROUP, GROUP)

    def turned(k):
        re, im, c, s = outer[0, k], outer[1, k], twist[0, k], twist[1, k]
        return re * c + im * s, im * c - re * s

    def step(k, carry):
        before_re, before_im, re, im = carry
        after_re, after_im = turned(k + 1)
        out_re = re - 0.5 * (before_re + after_re)
        out_im = im - 0.5 * (before_im + after_im)
        value = jnp.concatenate(
            [
                jnp.concatenate([out_re[:, :INNER], out_im[:, :INNER]], axis=1),
                jnp.concatenate([out_re[:, INNER:], out_im[:, INNER:]], axis=1),
            ],
            axis=0,
        )
        hi = value.astype(B16)
        g_hi[k, pl.ds(frame, GROUP), :] = hi
        g_lo[k, pl.ds(frame, GROUP), :] = (value - hi.astype(F32)).astype(B16)
        return re, im, after_re, after_im

    zero_re, zero_im = turned(0)
    one_re, one_im = turned(1)
    lax.fori_loop(0, HALF_K + 1, step, (one_re, -one_im, zero_re, zero_im), unroll=3)


def second_stage(second_hi, second_lo, g_hi, g_lo, mag):
    def magnitudes(lhs_hi, lhs_lo, hi, lo):
        out = dot_t(lhs_hi, hi) + dot_t(lhs_hi, lo) + dot_t(lhs_lo, hi)
        half = out.shape[0] // 2
        re, im = out[:half], out[half:]
        return jnp.sqrt(re * re + im * im)

    def put(at, a, b):
        rows = jnp.concatenate([a.reshape(NF, 8, FRAMES), b.reshape(NF, 8, FRAMES)], axis=1)
        mag[:, pl.ds(pl.multiple_of(at * 8, 16), 16), :] = rows.astype(B16)

    def halves(ref):
        return jnp.concatenate([ref[0:64], ref[128:192]], axis=0)

    def pair(p):
        hi = g_hi[pl.ds(2 * p, 2)].reshape(2 * FRAMES, 2 * INNER)
        lo = g_lo[pl.ds(2 * p, 2)].reshape(2 * FRAMES, 2 * INNER)
        return magnitudes(second_hi[...], second_lo[...], hi, lo)

    middle = magnitudes(halves(second_hi), halves(second_lo), g_hi[HALF_K], g_lo[HALF_K])
    out = pair(0)
    put(0, out[:64, :FRAMES], out[:64, FRAMES:])
    put(HALF_K, middle, out[64:, FRAMES:])

    def step(p, _):
        out = pair(p)
        put(2 * p, out[:64, :FRAMES], out[:64, FRAMES:])
        put(HALF_K + 2 * p, out[64:, :FRAMES], out[64:, FRAMES:])
        return 0

    lax.fori_loop(1, HALF_K // 2, step, 0)


def kernel(
    audio_hbm, w_ref, h_ref, first_hi, first_lo, twist, second_hi, second_lo, place,
    w_out, h_out,
    audio, outer, g_hi, g_lo, mag,
    gathered, blocks, comp, act,
    send_core, recv_core, send_plane, recv_plane,
    send_z, recv_z, full_z, numer, gram_rows, last,
    audio_sem, gather_sem, core_sems, plane_sem, z_sem, full_sem, wide_sem, fwd_sem, last_sem, act_sem,
):
    f, t = lax.axis_index("freq"), lax.axis_index("tm")
    y, c = lax.div(f, NC), lax.rem(f, NC)
    z, x = lax.div(t, NX), lax.rem(t, NX)
    q = y * NX + x
    span = 16 * FRAME

    def signal(freq, tm):
        pl.semaphore_signal(
            pltpu.get_barrier_semaphore(), inc=1, device_id={"freq": freq, "tm": tm},
            device_id_type=MESH,
        )

    def remote(src, dst, sems, freq, tm):
        return pltpu.make_async_remote_copy(
            src_ref=src, dst_ref=dst, send_sem=sems.at[0], recv_sem=sems.at[1],
            device_id={"freq": freq, "tm": tm}, device_id_type=MESH,
        )

    def drain(ref, sem):
        pltpu.make_async_copy(ref, ref, sem).wait()

    def plane_peer(i):
        other = lax.rem(q + i, NQ)
        return NC * lax.div(other, NX) + c, NX * z + lax.rem(other, NX)

    def z_peer(i):
        return lax.rem(z + i, NZ)

    def load(g):
        part = pl.ds(pl.multiple_of(g * span, span), span)
        return pltpu.make_async_copy(audio_hbm.at[:, part], audio.at[:, part], audio_sem.at[g])

    def each(low, high, body):
        def step(i, _):
            body(i)
            return 0

        lax.fori_loop(low, high, step, 0)

    each(0, GROUPS, lambda g: load(g).start())

    def greet_plane(i):
        signal(*plane_peer(i))

    def greet_z(i):
        signal(f, NX * z_peer(i) + x)

    def greet_other(i):
        signal(NC * i + (1 - c), t)

    each(1, NQ, greet_plane)
    each(1, NZ, greet_z)
    each(0, NY, greet_other)

    spread = dot(jnp.concatenate(terms(w_ref[...]), axis=0), place[...])
    spread = spread[:COMP] + spread[COMP : 2 * COMP] + spread[2 * COMP :]
    mine = c * NQ + y * NX
    for j in range(NX):
        block = spread[:, 128 * j : 128 * j + 128]
        blocks[j] = block
        gathered[0, mine + j] = gather_slot(block)
    comp[...] = blocks[x]
    act[...] = h_ref[:, pl.ds(pl.multiple_of(f * FRAMES, FRAMES), FRAMES)]

    def spectra(g):
        load(g).wait()
        first_stage(audio, first_hi, first_lo, twist, outer, g_hi, g_lo, g)

    each(0, GROUPS, spectra)

    pl.semaphore_wait(pltpu.get_barrier_semaphore(), (NQ - 1) + (NZ - 1) + NY)

    def send_start(i):
        slots = gathered.at[0, pl.ds(mine, NX)]
        remote(slots, slots, gather_sem, lax.rem(f + i, NF), t).start()

    each(1, NF, send_start)
    second_stage(second_hi, second_lo, g_hi, g_lo, mag)
    drain(gathered.at[0, pl.ds(0, (NF - 1) * NX)], gather_sem.at[1])

    for it in range(ITERS):
        def product(core):
            total = jnp.zeros((COMP, FRAMES), F32)
            for yy in range(NY):
                first = core * NQ + yy * NX
                rows = [gathered[it, first + j, :COMP, :] for j in range(NX)]
                total += dot(jnp.concatenate(rows, axis=1), mag[NC * yy + core])
            return total

        def gram_of(core):
            def add(i, total):
                tile = gathered[it, core * NQ + i, COMP:, :].astype(F32)
                return total + (tile[:8] + tile[8:])

            return lax.fori_loop(0, NQ, add, jnp.zeros((8, 128), F32), unroll=4)

        numer_h = product(c)
        gram_w = gram_of(c)
        if it == 1:
            drain(gathered.at[1, pl.ds(0, NQ)], fwd_sem.at[1])
        numer_h += product(1 - c)
        gram_w = unpack(gram_w + gram_of(1 - c))
        state = act[...]
        state = state * numer_h / dot(gram_w, state, HIGHEST)
        act[...] = state
        rounded = state.astype(B16)
        gram_h = pack(dot_t(state, state, HIGHEST))

        core_sem = core_sems.at[it]
        order = (2, 1, 3, 0)

        def partial(freq):
            return dot_t(rounded, mag[freq])

        for step, dy in enumerate(order):
            yy = lax.rem(y + dy, NY)
            value = partial(NC * yy + (1 - c))
            for j in range(NX):
                tile = jnp.concatenate([value[:, 128 * j : 128 * j + 128], gram_h], axis=0)
                send_core[it, yy * NX + j] = tile
            slots = pl.ds(yy * NX, NX)
            remote(
                send_core.at[it, slots], recv_core.at[it, slots], core_sem.at[step],
                NC * y + (1 - c), t,
            ).start()
        for step, dy in enumerate(order):
            yy = lax.rem(y + dy, NY)
            value = partial(NC * yy + c)
            drain(recv_core.at[it, pl.ds(yy * NX, NX)], core_sem.at[step, 1])
            for j in range(NX):
                slot = yy * NX + j
                tile = jnp.concatenate([value[:, 128 * j : 128 * j + 128], gram_h], axis=0)
                send_plane[it, slot] = tile + recv_core[it, slot]
            for dx in range(NX):
                xx = lax.rem(x + dx, NX)
                slot = yy * NX + xx
                if dy == 0 and dx == 0:
                    recv_plane[it, q] = send_plane[it, q]
                else:
                    remote(
                        send_plane.at[it, slot], recv_plane.at[it, q], plane_sem.at[it],
                        NC * yy + c, NX * z + xx,
                    ).start()

        if it == ITERS - 1:
            columns = pl.ds(pl.multiple_of(f * FRAMES, FRAMES), FRAMES)
            h_out[:, columns] = state

            def send_act(i):
                remote(act, h_out.at[:, columns], act_sem, lax.rem(f + i, NF), t).start()

            each(1, NF, send_act)

        drain(recv_plane.at[it, pl.ds(0, NQ - 1)], plane_sem.at[it, 1])
        total = recv_plane[it, 0]
        for i in range(1, NQ):
            total += recv_plane[it, i]
        for i in range(NZ):
            row = total[COMP + i // 2 : COMP + i // 2 + 1]
            send_z[it, i] = jnp.concatenate([total[2 * i : 2 * i + 2], row, row], axis=0)
        recv_z[it, z] = send_z[it, z]

        def scatter(i):
            zz = z_peer(i)
            remote(send_z.at[it, zz], recv_z.at[it, z], z_sem.at[it], f, NX * zz + x).start()

        each(1, NZ, scatter)
        drain(recv_z.at[it, pl.ds(0, NZ - 1)], z_sem.at[it, 1])
        part = recv_z[it, 0]
        for i in range(1, NZ):
            part += recv_z[it, i]
        full_z[it, z] = part

        def share(i):
            own = full_z.at[it, z]
            remote(own, own, full_sem.at[it], f, NX * z_peer(i) + x).start()

        each(1, NZ, share)
        drain(full_z.at[it, pl.ds(0, NZ - 1)], full_sem.at[it, 1])
        for i in range(NZ):
            numer[2 * i : 2 * i + 2, :] = full_z[it, i, 0:2, :]
            if i % 2 == 0:
                gram_rows[i // 2 : i // 2 + 1, :] = full_z[it, i, 2:3, :]
        own = comp[...]
        own = own * numer[...] / dot(unpack(gram_rows[...]), own, HIGHEST)
        comp[...] = own

        if it < ITERS - 1:
            at = c * NQ + q
            gathered[it + 1, at] = gather_slot(own)

            def spread_plane(i):
                slot = gathered.at[it + 1, at]
                remote(slot, slot, wide_sem, *plane_peer(i)).start()

            each(1, NQ, spread_plane)
            drain(gathered.at[it + 1, pl.ds(0, NQ - 1)], wide_sem.at[1])
            slots = gathered.at[it + 1, pl.ds(c * NQ, NQ)]
            remote(slots, slots, fwd_sem, NC * y + (1 - c), t).start()
        else:
            last[x] = own

            def spread_x(i):
                remote(comp, last.at[x], last_sem, f, NX * z + lax.rem(x + i, NX)).start()

            each(1, NX, spread_x)
            drain(last.at[pl.ds(0, NX - 1)], last_sem.at[1])

    whole = jnp.concatenate([last[j] for j in range(NX)], axis=1)
    whole = dot_t(jnp.concatenate(terms(whole), axis=0), place[...])
    w_out[...] = whole[:COMP] + whole[COMP : 2 * COMP] + whole[2 * COMP :]

    drain(h_out.at[:, pl.ds(0, (NF - 1) * FRAMES)], act_sem.at[1])
    drain(h_out.at[:, pl.ds(0, (NF - 1) * FRAMES)], act_sem.at[0])
    drain(gathered.at[0, pl.ds(0, (NF - 1) * NX)], gather_sem.at[0])
    drain(gathered.at[1, pl.ds(0, NQ - 1)], wide_sem.at[0])
    drain(gathered.at[1, pl.ds(0, NQ)], fwd_sem.at[0])
    drain(last.at[pl.ds(0, NX - 1)], last_sem.at[0])
    for it in range(ITERS):
        for step in range(NY):
            drain(send_core.at[it, pl.ds(0, NX)], core_sems.at[it, step, 0])
        drain(send_plane.at[it, pl.ds(0, NQ - 1)], plane_sem.at[it, 0])
        drain(send_z.at[it, pl.ds(0, NZ - 1)], z_sem.at[it, 0])
        drain(full_z.at[it, pl.ds(0, NZ - 1)], full_sem.at[it, 0])


def shards(audio, w_start, h_start):
    vmem = pl.BlockSpec(memory_space=pltpu.VMEM)
    dma = pltpu.SemaphoreType.DMA
    constants = [jnp.asarray(table) for table in tables()]
    return pl.pallas_call(
        kernel,
        out_shape=(
            jax.ShapeDtypeStruct((COMP, OWN), F32),
            jax.ShapeDtypeStruct((COMP, NF * FRAMES), F32),
        ),
        in_specs=[pl.BlockSpec(memory_space=pl.ANY)] + [vmem] * (2 + len(constants)),
        out_specs=(vmem, vmem),
        scratch_shapes=[
            pltpu.VMEM((1, FRAMES * FRAME), B16),
            pltpu.VMEM((2, NK, 8, 2 * INNER), F32),
            pltpu.VMEM((HALF_K + 1, FRAMES, 2 * INNER), B16),
            pltpu.VMEM((HALF_K + 1, FRAMES, 2 * INNER), B16),
            pltpu.VMEM((NF, OWN, FRAMES), B16),
            pltpu.VMEM((ITERS, NC * NQ, WROWS, 128), B16),
            pltpu.VMEM((NX, COMP, 128), F32),
            pltpu.VMEM((COMP, 128), F32),
            pltpu.VMEM((COMP, FRAMES), F32),
            pltpu.VMEM((ITERS, NQ, ROWS, 128), F32),
            pltpu.VMEM((ITERS, NQ, ROWS, 128), F32),
            pltpu.VMEM((ITERS, NQ, ROWS, 128), F32),
            pltpu.VMEM((ITERS, NQ, ROWS, 128), F32),
            pltpu.VMEM((ITERS, NZ, 4, 128), F32),
            pltpu.VMEM((ITERS, NZ, 4, 128), F32),
            pltpu.VMEM((ITERS, NZ, 4, 128), F32),
            pltpu.VMEM((COMP, 128), F32),
            pltpu.VMEM((8, 128), F32),
            pltpu.VMEM((NX, COMP, 128), F32),
            dma((GROUPS,)),
            dma((2,)),
            dma((ITERS, NY, 2)),
            dma((ITERS, 2)),
            dma((ITERS, 2)),
            dma((ITERS, 2)),
            dma((2,)),
            dma((2,)),
            dma((2,)),
            dma((2,)),
        ],
        compiler_params=pltpu.CompilerParams(
            collective_id=0, has_side_effects=True, vmem_limit_bytes=50 * 2**20
        ),
    )(audio, w_start, h_start, *constants)


def solution(mesh):
    placed = (P("tm", "freq"), P(None, "freq"), P(None, "tm"))
    return jax.shard_map(
        shards,
        mesh=mesh,
        in_specs=placed,
        out_specs=(P(None, "freq"), P(None, "tm")),
        check_vma=False,
    )
```

```python
import functools
import math

import jax
import jax.numpy as jnp
import ml_dtypes
import numpy as np
from jax import lax
from jax.experimental import pallas as pl
from jax.experimental.pallas import tpu as pltpu
from jax.sharding import PartitionSpec as P

MESH = pl.DeviceIdType.MESH
HIGHEST = lax.Precision.HIGHEST
F32 = jnp.float32
B16 = jnp.bfloat16

BINS = 4096
FRAME = 2 * BINS
ITERS = 2
COMP = 32
OUTER = 64
INNER = 128
NX, NY, NZ, NC = 4, 4, 16, 2
NF = NY * NC
NQ = NX * NY
OWN = BINS // NF
FRAMES = 128
GROUP = 16
GROUPS = FRAMES // GROUP
HALF_K = OUTER // 2
NK = HALF_K + 2
ROWS = COMP + 8
PACKED = COMP // 2 + 8
NS = 2 * NQ
HALF = 64


def two_terms(values):
    hi = values.astype(np.float32).astype(ml_dtypes.bfloat16)
    lo = (values - hi.astype(np.float64)).astype(np.float32).astype(ml_dtypes.bfloat16)
    return hi, lo


def tables():
    outer, inner, k = np.arange(OUTER), np.arange(INNER), np.arange(NK)
    angle = 2 * np.pi * (np.outer(k, outer) % OUTER) / OUTER
    first = np.zeros((2, NK, 8, 8, OUTER))
    for frame in range(8):
        first[0, :, frame, frame] = np.cos(angle)
        first[1, :, frame, frame] = -np.sin(angle)
    first_hi, first_lo = two_terms(first.reshape(2 * NK * 8, 8 * OUTER))
    angle = 2 * np.pi * np.outer(k, inner) / FRAME
    scale = 0.5 / math.sqrt(0.375 * FRAME)
    twist = np.stack([np.cos(angle) * scale, np.sin(angle) * scale])
    twist = np.concatenate([twist, twist], -1)[:, :, None, :]
    twist = np.ascontiguousarray(np.broadcast_to(twist, (2, NK, 8, 2 * INNER))).astype(np.float32)
    row = np.arange(INNER)
    second_k = np.where(row < 64, row, 191 - row)
    angle = 2 * np.pi * (np.outer(second_k, inner) % INNER) / INNER
    second_hi, second_lo = two_terms(
        np.block([[np.cos(angle), np.sin(angle)], [-np.sin(angle), np.cos(angle)]])
    )
    place = np.zeros((OWN, OWN), np.float32)
    for k1 in range(OUTER):
        at = k1 if k1 <= HALF_K else 3 * HALF_K - k1
        for k2 in range(8):
            place[OUTER * k2 + k1, at * 8 + k2] = 1.0
    return first_hi, first_lo, twist, second_hi, second_lo, place.astype(ml_dtypes.bfloat16)


def dot(a, b, precision=None):
    dims = (((1,), (0,)), ((), ()))
    return lax.dot_general(a, b, dims, precision=precision, preferred_element_type=F32)


def dot_t(a, b, precision=None):
    dims = (((1,), (1,)), ((), ()))
    return lax.dot_general(a, b, dims, precision=precision, preferred_element_type=F32)


def terms(value):
    hi = value.astype(B16)
    rest = value - hi.astype(F32)
    mid = rest.astype(B16)
    return hi, mid, (rest - mid.astype(F32)).astype(B16)


def pack(gram):
    return jnp.concatenate([gram[8 * i : 8 * i + 8] for i in range(4)], axis=1)


def unpack(tile):
    return jnp.concatenate([tile[:, 32 * i : 32 * i + 32] for i in range(4)], axis=0)


def swap(value):
    return jnp.concatenate([value[:, HALF:], value[:, :HALF]], axis=1)


def gather_slot(mine, block, gram):
    hi = gram.astype(B16).astype(F32)
    both = jnp.concatenate([hi, gram - hi], axis=1)
    return jnp.where(mine, block, jnp.concatenate([both, both], axis=1)).astype(B16)


def first_stage(audio, first_hi, first_lo, twist, outer, g_hi, g_lo, g):
    span = 8 * FRAME
    start = pl.multiple_of(g * (2 * span), 2 * span)
    left = audio[:, pl.ds(start, span)].reshape(8 * OUTER, INNER)
    right = audio[:, pl.ds(start + span, span)].reshape(8 * OUTER, INNER)
    both = jnp.concatenate([left, right], axis=1)
    outer[...] = (dot(first_hi[...], both) + dot(first_lo[...], both)).reshape(outer.shape)
    frame = pl.multiple_of(g * GROUP, GROUP)

    def turned(k):
        re, im, c, s = outer[0, k], outer[1, k], twist[0, k], twist[1, k]
        return re * c + im * s, im * c - re * s

    def step(k, carry):
        before_re, before_im, re, im = carry
        after_re, after_im = turned(k + 1)
        out_re = re - 0.5 * (before_re + after_re)
        out_im = im - 0.5 * (before_im + after_im)
        value = jnp.concatenate(
            [
                jnp.concatenate([out_re[:, :INNER], out_im[:, :INNER]], axis=1),
                jnp.concatenate([out_re[:, INNER:], out_im[:, INNER:]], axis=1),
            ],
            axis=0,
        )
        hi = value.astype(B16)
        g_hi[k, pl.ds(frame, GROUP), :] = hi
        g_lo[k, pl.ds(frame, GROUP), :] = (value - hi.astype(F32)).astype(B16)
        return re, im, after_re, after_im

    zero_re, zero_im = turned(0)
    one_re, one_im = turned(1)
    lax.fori_loop(0, HALF_K + 1, step, (one_re, -one_im, zero_re, zero_im), unroll=3)


def second_stage(second_hi, second_lo, g_hi, g_lo, mag):
    def magnitudes(lhs_hi, lhs_lo, hi, lo):
        out = dot_t(lhs_hi, hi) + dot_t(lhs_hi, lo) + dot_t(lhs_lo, hi)
        half = out.shape[0] // 2
        re, im = out[:half], out[half:]
        return jnp.sqrt(re * re + im * im)

    def put(at, a, b):
        rows = jnp.concatenate([a.reshape(NF, 8, FRAMES), b.reshape(NF, 8, FRAMES)], axis=1)
        mag[:, pl.ds(pl.multiple_of(at * 8, 16), 16), :] = rows.astype(B16)

    def halves(ref):
        return jnp.concatenate([ref[0:64], ref[128:192]], axis=0)

    def pair(p):
        hi = g_hi[pl.ds(2 * p, 2)].reshape(2 * FRAMES, 2 * INNER)
        lo = g_lo[pl.ds(2 * p, 2)].reshape(2 * FRAMES, 2 * INNER)
        return magnitudes(second_hi[...], second_lo[...], hi, lo)

    middle = magnitudes(halves(second_hi), halves(second_lo), g_hi[HALF_K], g_lo[HALF_K])
    out = pair(0)
    put(0, out[:64, :FRAMES], out[:64, FRAMES:])
    put(HALF_K, middle, out[64:, FRAMES:])

    def step(p, _):
        out = pair(p)
        put(2 * p, out[:64, :FRAMES], out[:64, FRAMES:])
        put(HALF_K + 2 * p, out[64:, :FRAMES], out[64:, FRAMES:])
        return 0

    lax.fori_loop(1, HALF_K // 2, step, 0)


def kernel(
    audio_hbm, w_hbm, h_hbm, first_hi_hbm, first_lo_hbm, twist_hbm, second_hi_hbm, second_lo_hbm,
    place_hbm,
    w_out, h_out,
    audio, w_in, h_in, first_hi, first_lo, twist, second_hi, second_lo, place,
    outer, g_hi, g_lo, mag,
    gathered, comp, act,
    send_core, recv_core, send_plane, recv_plane, sums, last,
    audio_sem, load_sem, gather_sem, core_sems, plane_sem, z_sem, wide_sem, fwd_sem, last_sem, act_sem,
):
    f, t = lax.axis_index("freq"), lax.axis_index("tm")
    y, c = lax.div(f, NC), lax.rem(f, NC)
    z, x = lax.div(t, NX), lax.rem(t, NX)
    far, m = lax.div(z, 2), lax.rem(z, 2)
    q = y * NX + x
    own_slot = 2 * q + m
    span = 16 * FRAME

    def signal(freq, tm):
        pl.semaphore_signal(
            pltpu.get_barrier_semaphore(), inc=1, device_id={"freq": freq, "tm": tm},
            device_id_type=MESH,
        )

    def remote(src, dst, sems, freq, tm):
        return pltpu.make_async_remote_copy(
            src_ref=src, dst_ref=dst, send_sem=sems.at[0], recv_sem=sems.at[1],
            device_id={"freq": freq, "tm": tm}, device_id_type=MESH,
        )

    def drain(ref, sem):
        pltpu.make_async_copy(ref, ref, sem).wait()

    def slot_device(slot):
        chip = lax.div(slot, 2)
        zz = z - m + lax.rem(slot, 2)
        return NC * lax.div(chip, NX) + c, NX * zz + lax.rem(chip, NX)

    def near_peer(i):
        return slot_device(lax.rem(own_slot + i, NS))

    def far_peer(i):
        return f, NX * (2 * lax.rem(far + i, NZ // 2) + m) + x

    def load_audio(g):
        part = pl.ds(pl.multiple_of(g * span, span), span)
        return pltpu.make_async_copy(audio_hbm.at[:, part], audio.at[:, part], audio_sem.at[g])

    def load(src, dst, i):
        return pltpu.make_async_copy(src, dst, load_sem.at[i])

    loads = [
        load(src, dst, i)
        for i, (src, dst) in enumerate(
            (
                (first_hi_hbm, first_hi),
                (first_lo_hbm, first_lo),
                (twist_hbm, twist),
                (w_hbm, w_in),
                (place_hbm, place),
                (second_hi_hbm, second_hi),
                (second_lo_hbm, second_lo),
                (h_hbm, h_in),
            )
        )
    ]

    def each(low, high, body):
        def step(i, _):
            body(i)
            return 0

        lax.fori_loop(low, high, step, 0)

    load_audio(0).start()
    for copy in loads[:3]:
        copy.start()
    each(1, NZ // 2, lambda i: signal(*far_peer(i)))
    each(1, NS, lambda i: signal(*near_peer(i)))
    each(0, NY, lambda i: signal(NC * i + (1 - c), t))
    each(1, GROUPS, lambda g: load_audio(g).start())
    for copy in loads[3:]:
        copy.start()
    for copy in loads[:3]:
        copy.wait()

    def spectra(g):
        load_audio(g).wait()
        first_stage(audio, first_hi, first_lo, twist, outer, g_hi, g_lo, g)

    each(0, GROUPS, spectra)

    for copy in loads[3:]:
        copy.wait()
    lane = lax.broadcasted_iota(jnp.int32, (COMP, 128), 1)
    low = lane < HALF
    mine = lax.div(lane, HALF) == m
    spread = dot(jnp.concatenate(terms(w_in[...]), axis=0), place[...])
    spread = spread[:COMP] + spread[COMP : 2 * COMP] + spread[2 * COMP :]
    gram = dot_t(spread, spread, HIGHEST)
    none = jnp.zeros_like(gram)
    first_slot = c * NS + 2 * NX * y
    for j in range(NX):
        block = spread[:, 128 * j : 128 * j + 128]
        last[2 * j] = block
        gathered[0, first_slot + 2 * j] = gather_slot(low, block, gram if j == 0 else none)
        gathered[0, first_slot + 2 * j + 1] = gather_slot(lane >= HALF, block, none)
    comp[...] = last[2 * x]
    act[...] = h_in[:, pl.ds(pl.multiple_of(f * FRAMES, FRAMES), FRAMES)]

    pl.semaphore_wait(pltpu.get_barrier_semaphore(), (NS - 1) + (NZ // 2 - 1) + NY)

    def send_start(i):
        slots = gathered.at[0, pl.ds(first_slot, 2 * NX)]
        remote(slots, slots, gather_sem, lax.rem(f + i, NF), t).start()

    each(1, NF, send_start)
    second_stage(second_hi, second_lo, g_hi, g_lo, mag)
    drain(gathered.at[0, pl.ds(0, (NF - 1) * 2 * NX)], gather_sem.at[1])

    for it in range(ITERS):
        def product(core):
            total = jnp.zeros((COMP, FRAMES), F32)
            for yy in range(NY):
                first = core * NS + 2 * NX * yy
                rows = [
                    jnp.where(low, gathered[it, first + 2 * j], gathered[it, first + 2 * j + 1])
                    for j in range(NX)
                ]
                total += dot(jnp.concatenate(rows, axis=1), mag[NC * yy + core])
            return total

        def gram_of(core):
            def add(i, total):
                at = core * NS + 2 * i
                return total + jnp.where(low, gathered[it, at + 1], gathered[it, at]).astype(F32)

            return lax.fori_loop(0, NQ, add, jnp.zeros((COMP, 128), F32), unroll=4)

        numer_h = product(c)
        gram_w = gram_of(c)
        if it == 1:
            drain(gathered.at[1, pl.ds(0, NS)], fwd_sem.at[1])
        numer_h += product(1 - c)
        gram_w += gram_of(1 - c)
        gram_w = (gram_w[:, :32] + gram_w[:, 64:96]) + (gram_w[:, 32:64] + gram_w[:, 96:])
        state = act[...]
        state = state * numer_h / dot(gram_w, state, HIGHEST)
        act[...] = state
        rounded = state.astype(B16)
        gram_h = pack(dot_t(state, state, HIGHEST))

        core_sem = core_sems.at[it]
        order = (2, 1, 3, 0)

        def partial(freq):
            return dot_t(rounded, mag[freq])

        for step, dy in enumerate(order):
            yy = lax.rem(y + dy, NY)
            value = partial(NC * yy + (1 - c))
            for j in range(NX):
                tile = jnp.concatenate([value[:, 128 * j : 128 * j + 128], gram_h], axis=0)
                send_core[it, yy * NX + j] = tile
            slots = pl.ds(yy * NX, NX)
            remote(
                send_core.at[it, slots], recv_core.at[it, slots], core_sem.at[step],
                NC * y + (1 - c), t,
            ).start()
        for step, dy in enumerate(order):
            yy = lax.rem(y + dy, NY)
            value = partial(NC * yy + c)
            drain(recv_core.at[it, pl.ds(yy * NX, NX)], core_sem.at[step, 1])
            for j in range(NX):
                chip = yy * NX + j
                tile = jnp.concatenate([value[:, 128 * j : 128 * j + 128], gram_h], axis=0)
                tile += recv_core[it, chip]
                top, bottom, sum_h = tile[:16], tile[16:32], tile[32:]
                left = jnp.where(low[:16], top, swap(bottom))
                right = jnp.where(low[:16], swap(top), bottom)
                send_plane[it, 2 * chip] = jnp.concatenate([left, sum_h], axis=0)
                send_plane[it, 2 * chip + 1] = jnp.concatenate([right, sum_h], axis=0)
            for dx in range(NX):
                xx = lax.rem(x + dx, NX)
                for dm in range(2):
                    slot = 2 * (yy * NX + xx) + lax.rem(m + dm, 2)
                    if dy == 0 and dx == 0 and dm == 0:
                        recv_plane[it, own_slot] = send_plane[it, own_slot]
                    else:
                        remote(
                            send_plane.at[it, slot], recv_plane.at[it, own_slot],
                            plane_sem.at[it], *slot_device(slot),
                        ).start()

        if it == ITERS - 1:
            columns = pl.ds(pl.multiple_of(f * FRAMES, FRAMES), FRAMES)
            h_out[:, columns] = state

            def send_act(i):
                remote(act, h_out.at[:, columns], act_sem, lax.rem(f + i, NF), t).start()

            each(1, NF, send_act)

        drain(recv_plane.at[it, pl.ds(0, NS - 1)], plane_sem.at[it, 1])
        total = recv_plane[it, 0]
        for i in range(1, NS):
            total += recv_plane[it, i]
        sums[it, far] = total

        def share(i):
            own = sums.at[it, far]
            remote(own, own, z_sem.at[it], *far_peer(i)).start()

        each(1, NZ // 2, share)
        drain(sums.at[it, pl.ds(0, NZ // 2 - 1)], z_sem.at[it, 1])
        total = sums[it, 0]
        for i in range(1, NZ // 2):
            total += sums[it, i]
        packed = total[:16]
        other = swap(packed)
        numer_w = jnp.concatenate(
            [jnp.where(m == 0, packed, other), jnp.where(m == 0, other, packed)], axis=0
        )
        own = comp[...]
        below = dot(unpack(total[16:]), own, HIGHEST)
        own = jnp.where(mine, own * numer_w / jnp.where(mine, below, 1.0), 0.0)
        comp[...] = own

        if it < ITERS - 1:
            at = c * NS + own_slot
            gathered[it + 1, at] = gather_slot(mine, own, dot_t(own, own, HIGHEST))

            def spread_near(i):
                slot = gathered.at[it + 1, at]
                remote(slot, slot, wide_sem, *near_peer(i)).start()

            each(1, NS, spread_near)
            drain(gathered.at[it + 1, pl.ds(0, NS - 1)], wide_sem.at[1])
            slots = gathered.at[it + 1, pl.ds(c * NS, NS)]
            remote(slots, slots, fwd_sem, NC * y + (1 - c), t).start()
        else:
            end = 2 * x + m
            last[end] = own

            def spread_x(i):
                peer = lax.rem(end + i, 2 * NX)
                zz = z - m + lax.rem(peer, 2)
                remote(comp, last.at[end], last_sem, f, NX * zz + lax.div(peer, 2)).start()

            each(1, 2 * NX, spread_x)
            drain(last.at[pl.ds(0, 2 * NX - 1)], last_sem.at[1])

    whole = [jnp.where(low, last[2 * j], last[2 * j + 1]) for j in range(NX)]
    whole = jnp.concatenate(whole, axis=1)
    whole = dot_t(jnp.concatenate(terms(whole), axis=0), place[...])
    w_out[...] = whole[:COMP] + whole[COMP : 2 * COMP] + whole[2 * COMP :]

    drain(h_out.at[:, pl.ds(0, (NF - 1) * FRAMES)], act_sem.at[1])
    drain(h_out.at[:, pl.ds(0, (NF - 1) * FRAMES)], act_sem.at[0])
    drain(gathered.at[0, pl.ds(0, (NF - 1) * 2 * NX)], gather_sem.at[0])
    drain(gathered.at[1, pl.ds(0, NS - 1)], wide_sem.at[0])
    drain(gathered.at[1, pl.ds(0, NS)], fwd_sem.at[0])
    drain(last.at[pl.ds(0, 2 * NX - 1)], last_sem.at[0])
    for it in range(ITERS):
        for step in range(NY):
            drain(send_core.at[it, pl.ds(0, NX)], core_sems.at[it, step, 0])
        drain(send_plane.at[it, pl.ds(0, NS - 1)], plane_sem.at[it, 0])
        drain(sums.at[it, pl.ds(0, NZ // 2 - 1)], z_sem.at[it, 0])


def shards(audio, w_start, h_start):
    vmem = pl.BlockSpec(memory_space=pltpu.VMEM)
    dma = pltpu.SemaphoreType.DMA
    constants = [jnp.asarray(table) for table in tables()]
    operands = (audio, w_start, h_start, *constants)
    return pl.pallas_call(
        kernel,
        out_shape=(
            jax.ShapeDtypeStruct((COMP, OWN), F32),
            jax.ShapeDtypeStruct((COMP, NF * FRAMES), F32),
        ),
        in_specs=[pl.BlockSpec(memory_space=pltpu.HBM)] * len(operands),
        out_specs=(vmem, vmem),
        scratch_shapes=[
            *(pltpu.VMEM(operand.shape, operand.dtype) for operand in operands),
            pltpu.VMEM((2, NK, 8, 2 * INNER), F32),
            pltpu.VMEM((HALF_K + 1, FRAMES, 2 * INNER), B16),
            pltpu.VMEM((HALF_K + 1, FRAMES, 2 * INNER), B16),
            pltpu.VMEM((NF, OWN, FRAMES), B16),
            pltpu.VMEM((ITERS, NC * NS, COMP, 128), B16),
            pltpu.VMEM((COMP, 128), F32),
            pltpu.VMEM((COMP, FRAMES), F32),
            pltpu.VMEM((ITERS, NQ, ROWS, 128), F32),
            pltpu.VMEM((ITERS, NQ, ROWS, 128), F32),
            pltpu.VMEM((ITERS, NS, PACKED, 128), F32),
            pltpu.VMEM((ITERS, NS, PACKED, 128), F32),
            pltpu.VMEM((ITERS, NZ // 2, PACKED, 128), F32),
            pltpu.VMEM((2 * NX, COMP, 128), F32),
            dma((GROUPS,)),
            dma((8,)),
            dma((2,)),
            dma((ITERS, NY, 2)),
            dma((ITERS, 2)),
            dma((ITERS, 2)),
            dma((2,)),
            dma((2,)),
            dma((2,)),
            dma((2,)),
        ],
        compiler_params=pltpu.CompilerParams(
            collective_id=0, has_side_effects=True, vmem_limit_bytes=64 * 2**20 - 2**16
        ),
    )(*operands)


def solution(mesh):
    placed = (P("tm", "freq"), P(None, "freq"), P(None, "tm"))
    return jax.shard_map(
        shards,
        mesh=mesh,
        in_specs=placed,
        out_specs=(P(None, "freq"), P(None, "tm")),
        check_vma=False,
    )
```

```python
import functools
import math

import jax
import jax.numpy as jnp
import ml_dtypes
import numpy as np
from jax import lax
from jax.experimental import pallas as pl
from jax.experimental.pallas import tpu as pltpu
from jax.sharding import PartitionSpec as P

MESH = pl.DeviceIdType.MESH
HIGHEST = lax.Precision.HIGHEST
F32 = jnp.float32
B16 = jnp.bfloat16

BINS = 4096
FRAME = 2 * BINS
ITERS = 2
COMP = 32
OUTER = 64
INNER = 128
NX, NY, NZ, NC = 4, 4, 16, 2
NF = NY * NC
NQ = NX * NY
OWN = BINS // NF
FRAMES = 128
GROUP = 16
GROUPS = FRAMES // GROUP
HALF_K = OUTER // 2
NK = HALF_K + 2
PACKED = COMP // 2
EARLY = 4
START = NX * COMP + 16
NS = 2 * NQ
HALF = 64


def two_terms(values):
    hi = values.astype(np.float32).astype(ml_dtypes.bfloat16)
    lo = (values - hi.astype(np.float64)).astype(np.float32).astype(ml_dtypes.bfloat16)
    return hi, lo


def tables():
    outer, inner, k = np.arange(OUTER), np.arange(INNER), np.arange(NK)
    angle = 2 * np.pi * (np.outer(k, outer) % OUTER) / OUTER
    first = np.zeros((2, NK, 8, 8, OUTER))
    for frame in range(8):
        first[0, :, frame, frame] = np.cos(angle)
        first[1, :, frame, frame] = -np.sin(angle)
    first_hi, first_lo = two_terms(first.reshape(2 * NK * 8, 8 * OUTER))
    angle = 2 * np.pi * np.outer(k, inner) / FRAME
    scale = 0.5 / math.sqrt(0.375 * FRAME)
    twist = np.stack([np.cos(angle) * scale, np.sin(angle) * scale])
    twist = np.concatenate([twist, twist], -1)[:, :, None, :]
    twist = np.ascontiguousarray(np.broadcast_to(twist, (2, NK, 8, 2 * INNER))).astype(np.float32)
    row = np.arange(INNER)
    second_k = np.where(row < 64, row, 191 - row)
    angle = 2 * np.pi * (np.outer(second_k, inner) % INNER) / INNER
    second_hi, second_lo = two_terms(
        np.block([[np.cos(angle), np.sin(angle)], [-np.sin(angle), np.cos(angle)]])
    )
    place = np.zeros((OWN, OWN), np.float32)
    for k1 in range(OUTER):
        at = k1 if k1 <= HALF_K else 3 * HALF_K - k1
        for k2 in range(8):
            place[OUTER * k2 + k1, at * 8 + k2] = 1.0
    return first_hi, first_lo, twist, second_hi, second_lo, place.astype(ml_dtypes.bfloat16)


def dot(a, b, precision=None):
    dims = (((1,), (0,)), ((), ()))
    return lax.dot_general(a, b, dims, precision=precision, preferred_element_type=F32)


def dot_t(a, b, precision=None):
    dims = (((1,), (1,)), ((), ()))
    return lax.dot_general(a, b, dims, precision=precision, preferred_element_type=F32)


def terms(value):
    hi = value.astype(B16)
    rest = value - hi.astype(F32)
    mid = rest.astype(B16)
    return hi, mid, (rest - mid.astype(F32)).astype(B16)


def pack(gram):
    return jnp.concatenate([gram[8 * i : 8 * i + 8] for i in range(4)], axis=1)


def unpack(tile):
    return jnp.concatenate([tile[:, 32 * i : 32 * i + 32] for i in range(4)], axis=0)


def swap(value):
    return jnp.concatenate([value[:, HALF:], value[:, :HALF]], axis=1)


def gather_slot(mine, block, gram):
    hi = gram.astype(B16).astype(F32)
    both = jnp.concatenate([hi, gram - hi], axis=1)
    return jnp.where(mine, block, jnp.concatenate([both, both], axis=1)).astype(B16)


def first_stage(audio, first_hi, first_lo, twist, outer, g_hi, g_lo, g):
    span = 8 * FRAME
    start = pl.multiple_of(g * (2 * span), 2 * span)
    left = audio[:, pl.ds(start, span)].reshape(8 * OUTER, INNER)
    right = audio[:, pl.ds(start + span, span)].reshape(8 * OUTER, INNER)
    both = jnp.concatenate([left, right], axis=1)
    outer = outer.at[lax.rem(g, 2)]
    outer[...] = (dot(first_hi[...], both) + dot(first_lo[...], both)).reshape(outer.shape)
    frame = pl.multiple_of(g * GROUP, GROUP)

    def turned(k):
        re, im, c, s = outer[0, k], outer[1, k], twist[0, k], twist[1, k]
        return re * c + im * s, im * c - re * s

    def step(k, carry):
        before_re, before_im, re, im = carry
        after_re, after_im = turned(k + 1)
        out_re = re - 0.5 * (before_re + after_re)
        out_im = im - 0.5 * (before_im + after_im)
        value = jnp.concatenate(
            [
                jnp.concatenate([out_re[:, :INNER], out_im[:, :INNER]], axis=1),
                jnp.concatenate([out_re[:, INNER:], out_im[:, INNER:]], axis=1),
            ],
            axis=0,
        )
        hi = value.astype(B16)
        g_hi[k, pl.ds(frame, GROUP), :] = hi
        g_lo[k, pl.ds(frame, GROUP), :] = (value - hi.astype(F32)).astype(B16)
        return re, im, after_re, after_im

    zero_re, zero_im = turned(0)
    one_re, one_im = turned(1)
    lax.fori_loop(0, HALF_K + 1, step, (one_re, -one_im, zero_re, zero_im), unroll=True)


def second_stage(second_hi, second_lo, g_hi, g_lo, mag):
    def magnitudes(lhs_hi, lhs_lo, hi, lo):
        out = dot_t(lhs_hi, hi) + dot_t(lhs_hi, lo) + dot_t(lhs_lo, hi)
        half = out.shape[0] // 2
        re, im = out[:half], out[half:]
        return jnp.sqrt(re * re + im * im)

    def put(at, a, b):
        rows = jnp.concatenate([a.reshape(NF, 8, FRAMES), b.reshape(NF, 8, FRAMES)], axis=1)
        mag[:, pl.ds(pl.multiple_of(at * 8, 16), 16), :] = rows.astype(B16)

    def halves(ref):
        return jnp.concatenate([ref[0:64], ref[128:192]], axis=0)

    def pair(p):
        hi = g_hi[pl.ds(2 * p, 2)].reshape(2 * FRAMES, 2 * INNER)
        lo = g_lo[pl.ds(2 * p, 2)].reshape(2 * FRAMES, 2 * INNER)
        return magnitudes(second_hi[...], second_lo[...], hi, lo)

    middle = magnitudes(halves(second_hi), halves(second_lo), g_hi[HALF_K], g_lo[HALF_K])
    out = pair(0)
    put(0, out[:64, :FRAMES], out[:64, FRAMES:])
    put(HALF_K, middle, out[64:, FRAMES:])

    def step(p, _):
        out = pair(p)
        put(2 * p, out[:64, :FRAMES], out[:64, FRAMES:])
        put(HALF_K + 2 * p, out[64:, :FRAMES], out[64:, FRAMES:])
        return 0

    lax.fori_loop(1, HALF_K // 2, step, 0, unroll=True)


def kernel(
    audio_hbm, w_hbm, h_hbm, first_hi_hbm, first_lo_hbm, twist_hbm, second_hi_hbm, second_lo_hbm,
    place_hbm,
    w_out, h_out,
    audio, w_in, h_in, first_hi, first_lo, twist, second_hi, second_lo, place,
    outer, g_hi, g_lo, mag,
    start, gathered, comp, act,
    send_core, recv_core, send_plane, recv_plane, sums, last,
    gram_mine, gram_core, gram_z, gram_plane,
    audio_sem, load_sem, gather_sem, core_sems, plane_sem, z_sem, wide_sem, fwd_sem, last_sem, act_sem,
    gram_core_sem, gram_z_sem, gram_plane_sem,
):
    f, t = lax.axis_index("freq"), lax.axis_index("tm")
    y, c = lax.div(f, NC), lax.rem(f, NC)
    z, x = lax.div(t, NX), lax.rem(t, NX)
    far, m = lax.div(z, 2), lax.rem(z, 2)
    q = y * NX + x
    own_slot = 2 * q + m
    span = 16 * FRAME

    def signal(freq, tm):
        pl.semaphore_signal(
            pltpu.get_barrier_semaphore(), inc=1, device_id={"freq": freq, "tm": tm},
            device_id_type=MESH,
        )

    def remote(src, dst, sems, freq, tm):
        return pltpu.make_async_remote_copy(
            src_ref=src, dst_ref=dst, send_sem=sems.at[0], recv_sem=sems.at[1],
            device_id={"freq": freq, "tm": tm}, device_id_type=MESH,
        )

    def drain(ref, sem):
        pltpu.make_async_copy(ref, ref, sem).wait()

    def slot_device(slot):
        chip = lax.div(slot, 2)
        zz = z - m + lax.rem(slot, 2)
        return NC * lax.div(chip, NX) + c, NX * zz + lax.rem(chip, NX)

    def near_peer(i):
        return slot_device(lax.rem(own_slot + i, NS))

    def far_peer(i):
        return f, NX * (2 * lax.rem(far + i, NZ // 2) + m) + x

    def z_peer(i):
        return f, NX * lax.rem(z + i, NZ) + x

    def plane_peer(i):
        return slot_device(2 * lax.rem(q + i, NQ) + m)

    def load_audio(g):
        part = pl.ds(pl.multiple_of(g * span, span), span)
        return pltpu.make_async_copy(audio_hbm.at[:, part], audio.at[:, part], audio_sem.at[g])

    def load(src, dst, i):
        return pltpu.make_async_copy(src, dst, load_sem.at[i])

    loads = [
        load(src, dst, i)
        for i, (src, dst) in enumerate(
            (
                (first_hi_hbm, first_hi),
                (first_lo_hbm, first_lo),
                (twist_hbm, twist),
                (w_hbm, w_in),
                (place_hbm, place),
                (second_hi_hbm, second_hi),
                (second_lo_hbm, second_lo),
                (h_hbm, h_in),
            )
        )
    ]

    def each(low, high, body):
        def step(i, _):
            body(i)
            return 0

        lax.fori_loop(low, high, step, 0)

    load_audio(0).start()
    for copy in loads[:3]:
        copy.start()
    each(1, NZ // 2, lambda i: signal(*far_peer(i)))
    each(1, NZ // 2, lambda i: signal(f, NX * (2 * lax.rem(far + i, NZ // 2) + 1 - m) + x))
    each(1, NS, lambda i: signal(*near_peer(i)))
    each(0, NY, lambda i: signal(NC * i + (1 - c), t))
    each(1, GROUPS, lambda g: load_audio(g).start())
    for copy in loads[3:]:
        copy.start()
    for copy in loads[:3]:
        copy.wait()

    def spectra(p):
        for g in (2 * p, 2 * p + 1):
            load_audio(g).wait()
        for g in (2 * p, 2 * p + 1):
            first_stage(audio, first_hi, first_lo, twist, outer, g_hi, g_lo, g)

    each(0, EARLY // 2, spectra)

    for copy in loads[3:]:
        copy.wait()
    lane = lax.broadcasted_iota(jnp.int32, (COMP, 128), 1)
    low = lane < HALF
    mine = lax.div(lane, HALF) == m
    spread = dot(jnp.concatenate(terms(w_in[...]), axis=0), place[...])
    spread = spread[:COMP] + spread[COMP : 2 * COMP] + spread[2 * COMP :]
    gram = dot_t(spread, spread, HIGHEST)
    gram = pack(gram)
    hi = gram.astype(B16).astype(F32)
    start[f, NX * COMP :, :] = jnp.concatenate([hi, gram - hi], axis=0).astype(B16)
    for j in range(NX):
        block = spread[:, 128 * j : 128 * j + 128]
        last[2 * j] = block
        start[f, COMP * j : COMP * j + COMP, :] = block.astype(B16)
    comp[...] = last[2 * x]
    act[...] = h_in[:, pl.ds(pl.multiple_of(f * FRAMES, FRAMES), FRAMES)]

    pl.semaphore_wait(pltpu.get_barrier_semaphore(), (NS - 1) + 2 * (NZ // 2 - 1) + NY)

    def send_start(i):
        remote(start.at[f], start.at[f], gather_sem, lax.rem(f + i, NF), t).start()

    each(1, NF, send_start)
    each(EARLY // 2, GROUPS // 2, spectra)
    second_stage(second_hi, second_lo, g_hi, g_lo, mag)
    drain(start.at[pl.ds(0, NF - 1)], gather_sem.at[1])

    for it in range(ITERS):
        def product(core):
            total = jnp.zeros((COMP, FRAMES), F32)
            for yy in range(NY):
                if it == 0:
                    rows = [start[NC * yy + core, COMP * j : COMP * j + COMP, :] for j in range(NX)]
                else:
                    first = core * NS + 2 * NX * yy
                    rows = [
                        jnp.where(low, gathered[first + 2 * j], gathered[first + 2 * j + 1])
                        for j in range(NX)
                    ]
                total += dot(jnp.concatenate(rows, axis=1), mag[NC * yy + core])
            return total

        def gram_of(core):
            total = jnp.zeros((COMP, 128), F32)

            def add(i, total):
                at = core * NS + 2 * i
                return total + jnp.where(low, gathered[at + 1], gathered[at]).astype(F32)

            return lax.fori_loop(0, NQ, add, total, unroll=4)

        numer_h = product(c)
        gram_w = gram_of(c) if it > 0 else None
        if it == 1:
            drain(gathered.at[pl.ds(0, NS)], fwd_sem.at[1])
        numer_h += product(1 - c)
        if it == 0:
            total = start[0, NX * COMP :, :].astype(F32)
            for i in range(1, NF):
                total += start[i, NX * COMP :, :].astype(F32)
            gram_w = unpack(total[:8] + total[8:])
        else:
            gram_w += gram_of(1 - c)
            gram_w = (gram_w[:, :32] + gram_w[:, 64:96]) + (gram_w[:, 32:64] + gram_w[:, 96:])
        state = act[...]
        state = state * numer_h / dot(gram_w, state, HIGHEST)
        act[...] = state
        rounded = state.astype(B16)
        gram_mine[it] = pack(dot_t(state, state, HIGHEST))
        remote(
            gram_mine.at[it], gram_core.at[it], gram_core_sem.at[it], NC * y + (1 - c), t
        ).start()

        core_sem = core_sems.at[it]
        order = (2, 1, 3, 0)

        def partial(freq):
            return dot_t(rounded, mag[freq])

        for step, dy in enumerate(order):
            yy = lax.rem(y + dy, NY)
            value = partial(NC * yy + (1 - c))
            for j in range(NX):
                send_core[it, yy * NX + j] = value[:, 128 * j : 128 * j + 128]
            slots = pl.ds(yy * NX, NX)
            remote(
                send_core.at[it, slots], recv_core.at[it, slots], core_sem.at[step],
                NC * y + (1 - c), t,
            ).start()
        for step, dy in enumerate(order):
            yy = lax.rem(y + dy, NY)
            value = partial(NC * yy + c)
            drain(recv_core.at[it, pl.ds(yy * NX, NX)], core_sem.at[step, 1])
            for j in range(NX):
                chip = yy * NX + j
                tile = value[:, 128 * j : 128 * j + 128] + recv_core[it, chip]
                top, bottom = tile[:PACKED], tile[PACKED:]
                send_plane[it, 2 * chip] = jnp.where(low[:PACKED], top, swap(bottom))
                send_plane[it, 2 * chip + 1] = jnp.where(low[:PACKED], swap(top), bottom)
            for dx in range(NX):
                xx = lax.rem(x + dx, NX)
                for dm in range(2):
                    slot = 2 * (yy * NX + xx) + lax.rem(m + dm, 2)
                    if dy == 0 and dx == 0 and dm == 0:
                        recv_plane[it, own_slot] = send_plane[it, own_slot]
                    else:
                        remote(
                            send_plane.at[it, slot], recv_plane.at[it, own_slot],
                            plane_sem.at[it], *slot_device(slot),
                        ).start()

        drain(gram_core.at[it], gram_core_sem.at[it, 1])
        gram_z[it, z] = gram_mine[it] + gram_core[it]

        def gram_to_z(i):
            own = gram_z.at[it, z]
            remote(own, own, gram_z_sem.at[it], *z_peer(i)).start()

        each(1, NZ, gram_to_z)

        drain(recv_plane.at[it, pl.ds(0, NS - 1)], plane_sem.at[it, 1])
        total = recv_plane[it, 0]
        for i in range(1, NS):
            total += recv_plane[it, i]
        sums[it, far] = total

        def share(i):
            own = sums.at[it, far]
            remote(own, own, z_sem.at[it], *far_peer(i)).start()

        each(1, NZ // 2, share)
        drain(gram_z.at[it, pl.ds(0, NZ - 1)], gram_z_sem.at[it, 1])
        gram_h = gram_z[it, 0]
        for i in range(1, NZ):
            gram_h += gram_z[it, i]
        gram_plane[it, q] = gram_h

        def gram_to_plane(i):
            own = gram_plane.at[it, q]
            remote(own, own, gram_plane_sem.at[it], *plane_peer(i)).start()

        each(1, NQ, gram_to_plane)
        if it == ITERS - 1:
            columns = pl.ds(pl.multiple_of(f * FRAMES, FRAMES), FRAMES)
            h_out[:, columns] = state

            def send_act(i):
                remote(act, h_out.at[:, columns], act_sem, lax.rem(f + i, NF), t).start()

            each(1, NF, send_act)

        drain(sums.at[it, pl.ds(0, NZ // 2 - 1)], z_sem.at[it, 1])
        total = sums[it, 0]
        for i in range(1, NZ // 2):
            total += sums[it, i]
        drain(gram_plane.at[it, pl.ds(0, NQ - 1)], gram_plane_sem.at[it, 1])
        gram_h = gram_plane[it, 0]
        for i in range(1, NQ):
            gram_h += gram_plane[it, i]
        packed = total
        other = swap(packed)
        numer_w = jnp.concatenate(
            [jnp.where(m == 0, packed, other), jnp.where(m == 0, other, packed)], axis=0
        )
        own = comp[...]
        below = dot(unpack(gram_h), own, HIGHEST)
        own = jnp.where(mine, own * numer_w / jnp.where(mine, below, 1.0), 0.0)
        comp[...] = own

        if it < ITERS - 1:
            at = c * NS + own_slot
            gathered[at] = gather_slot(mine, own, dot_t(own, own, HIGHEST))

            def spread_near(i):
                slot = gathered.at[at]
                remote(slot, slot, wide_sem, *near_peer(i)).start()

            each(1, NS, spread_near)
            drain(gathered.at[pl.ds(0, NS - 1)], wide_sem.at[1])
            slots = gathered.at[pl.ds(c * NS, NS)]
            remote(slots, slots, fwd_sem, NC * y + (1 - c), t).start()
        else:
            end = 2 * x + m
            last[end] = own

            def spread_x(i):
                peer = lax.rem(end + i, 2 * NX)
                zz = z - m + lax.rem(peer, 2)
                remote(comp, last.at[end], last_sem, f, NX * zz + lax.div(peer, 2)).start()

            each(1, 2 * NX, spread_x)
            drain(last.at[pl.ds(0, 2 * NX - 1)], last_sem.at[1])

    whole = [jnp.where(low, last[2 * j], last[2 * j + 1]) for j in range(NX)]
    whole = jnp.concatenate(whole, axis=1)
    whole = dot_t(jnp.concatenate(terms(whole), axis=0), place[...])
    w_out[...] = whole[:COMP] + whole[COMP : 2 * COMP] + whole[2 * COMP :]

    drain(h_out.at[:, pl.ds(0, (NF - 1) * FRAMES)], act_sem.at[1])
    drain(h_out.at[:, pl.ds(0, (NF - 1) * FRAMES)], act_sem.at[0])
    drain(start.at[pl.ds(0, NF - 1)], gather_sem.at[0])
    drain(gathered.at[pl.ds(0, NS - 1)], wide_sem.at[0])
    drain(gathered.at[pl.ds(0, NS)], fwd_sem.at[0])
    drain(last.at[pl.ds(0, 2 * NX - 1)], last_sem.at[0])
    for it in range(ITERS):
        for step in range(NY):
            drain(send_core.at[it, pl.ds(0, NX)], core_sems.at[it, step, 0])
        drain(send_plane.at[it, pl.ds(0, NS - 1)], plane_sem.at[it, 0])
        drain(sums.at[it, pl.ds(0, NZ // 2 - 1)], z_sem.at[it, 0])
        drain(gram_mine.at[it], gram_core_sem.at[it, 0])
        drain(gram_z.at[it, pl.ds(0, NZ - 1)], gram_z_sem.at[it, 0])
        drain(gram_plane.at[it, pl.ds(0, NQ - 1)], gram_plane_sem.at[it, 0])


def shards(audio, w_start, h_start):
    vmem = pl.BlockSpec(memory_space=pltpu.VMEM)
    dma = pltpu.SemaphoreType.DMA
    constants = [jnp.asarray(table) for table in tables()]
    operands = (audio, w_start, h_start, *constants)
    return pl.pallas_call(
        kernel,
        out_shape=(
            jax.ShapeDtypeStruct((COMP, OWN), F32),
            jax.ShapeDtypeStruct((COMP, NF * FRAMES), F32),
        ),
        in_specs=[pl.BlockSpec(memory_space=pltpu.HBM)] * len(operands),
        out_specs=(vmem, vmem),
        scratch_shapes=[
            *(pltpu.VMEM(operand.shape, operand.dtype) for operand in operands),
            pltpu.VMEM((2, 2, NK, 8, 2 * INNER), F32),
            pltpu.VMEM((HALF_K + 1, FRAMES, 2 * INNER), B16),
            pltpu.VMEM((HALF_K + 1, FRAMES, 2 * INNER), B16),
            pltpu.VMEM((NF, OWN, FRAMES), B16),
            pltpu.VMEM((NF, START, 128), B16),
            pltpu.VMEM((NC * NS, COMP, 128), B16),
            pltpu.VMEM((COMP, 128), F32),
            pltpu.VMEM((COMP, FRAMES), F32),
            pltpu.VMEM((ITERS, NQ, COMP, 128), F32),
            pltpu.VMEM((ITERS, NQ, COMP, 128), F32),
            pltpu.VMEM((ITERS, NS, PACKED, 128), F32),
            pltpu.VMEM((ITERS, NS, PACKED, 128), F32),
            pltpu.VMEM((ITERS, NZ // 2, PACKED, 128), F32),
            pltpu.VMEM((2 * NX, COMP, 128), F32),
            pltpu.VMEM((ITERS, 8, 128), F32),
            pltpu.VMEM((ITERS, 8, 128), F32),
            pltpu.VMEM((ITERS, NZ, 8, 128), F32),
            pltpu.VMEM((ITERS, NQ, 8, 128), F32),
            dma((GROUPS,)),
            dma((8,)),
            dma((2,)),
            dma((ITERS, NY, 2)),
            dma((ITERS, 2)),
            dma((ITERS, 2)),
            dma((2,)),
            dma((2,)),
            dma((2,)),
            dma((2,)),
            dma((ITERS, 2)),
            dma((ITERS, 2)),
            dma((ITERS, 2)),
        ],
        compiler_params=pltpu.CompilerParams(
            collective_id=0, has_side_effects=True, vmem_limit_bytes=64 * 2**20 - 2**16
        ),
    )(*operands)


def solution(mesh):
    placed = (P("tm", "freq"), P(None, "freq"), P(None, "tm"))
    return jax.shard_map(
        shards,
        mesh=mesh,
        in_specs=placed,
        out_specs=(P(None, "freq"), P(None, "tm")),
        check_vma=False,
    )
```

```python
import functools
import math

import jax
import jax.numpy as jnp
import ml_dtypes
import numpy as np
from jax import lax
from jax.experimental import pallas as pl
from jax.experimental.pallas import tpu as pltpu
from jax.sharding import PartitionSpec as P

MESH = pl.DeviceIdType.MESH
HIGHEST = lax.Precision.HIGHEST
F32 = jnp.float32
B16 = jnp.bfloat16

BINS = 4096
FRAME = 2 * BINS
ITERS = 2
COMP = 32
OUTER = 64
INNER = 128
NX, NY, NZ, NC = 4, 4, 16, 2
NF = NY * NC
NQ = NX * NY
OWN = BINS // NF
FRAMES = 128
GROUP = 16
GROUPS = FRAMES // GROUP
HALF_K = OUTER // 2
NK = HALF_K + 2
PACKED = COMP // 2
EARLY = 4
START = NX * COMP + 16
NS = 2 * NQ
HALF = 64


def two_terms(values):
    hi = values.astype(np.float32).astype(ml_dtypes.bfloat16)
    lo = (values - hi.astype(np.float64)).astype(np.float32).astype(ml_dtypes.bfloat16)
    return hi, lo


def tables():
    outer, inner, k = np.arange(OUTER), np.arange(INNER), np.arange(NK)
    angle = 2 * np.pi * (np.outer(k, outer) % OUTER) / OUTER
    first = np.zeros((2, NK, 8, 8, OUTER))
    for frame in range(8):
        first[0, :, frame, frame] = np.cos(angle)
        first[1, :, frame, frame] = -np.sin(angle)
    first_hi, first_lo = two_terms(first.reshape(2 * NK * 8, 8 * OUTER))
    angle = 2 * np.pi * np.outer(k, inner) / FRAME
    scale = 0.5 / math.sqrt(0.375 * FRAME)
    twist = np.stack([np.cos(angle) * scale, np.sin(angle) * scale])
    twist = np.concatenate([twist, twist], -1)[:, :, None, :]
    twist = np.ascontiguousarray(np.broadcast_to(twist, (2, NK, 8, 2 * INNER))).astype(np.float32)
    row = np.arange(INNER)
    second_k = np.where(row < 64, row, 191 - row)
    angle = 2 * np.pi * (np.outer(second_k, inner) % INNER) / INNER
    second_hi, second_lo = two_terms(
        np.block([[np.cos(angle), np.sin(angle)], [-np.sin(angle), np.cos(angle)]])
    )
    place = np.zeros((OWN, OWN), np.float32)
    for k1 in range(OUTER):
        at = k1 if k1 <= HALF_K else 3 * HALF_K - k1
        for k2 in range(8):
            place[OUTER * k2 + k1, at * 8 + k2] = 1.0
    return first_hi, first_lo, twist, second_hi, second_lo, place.astype(ml_dtypes.bfloat16)


def dot(a, b, precision=None):
    dims = (((1,), (0,)), ((), ()))
    return lax.dot_general(a, b, dims, precision=precision, preferred_element_type=F32)


def dot_t(a, b, precision=None):
    dims = (((1,), (1,)), ((), ()))
    return lax.dot_general(a, b, dims, precision=precision, preferred_element_type=F32)


def terms(value):
    hi = value.astype(B16)
    rest = value - hi.astype(F32)
    mid = rest.astype(B16)
    return hi, mid, (rest - mid.astype(F32)).astype(B16)


def pack(gram):
    return jnp.concatenate([gram[8 * i : 8 * i + 8] for i in range(4)], axis=1)


def unpack(tile):
    return jnp.concatenate([tile[:, 32 * i : 32 * i + 32] for i in range(4)], axis=0)


def swap(value):
    return jnp.concatenate([value[:, HALF:], value[:, :HALF]], axis=1)


def gather_slot(mine, block, gram):
    hi = gram.astype(B16).astype(F32)
    both = jnp.concatenate([hi, gram - hi], axis=1)
    return jnp.where(mine, block, jnp.concatenate([both, both], axis=1)).astype(B16)


def first_stage(audio, first_hi, first_lo, twist, outer, g_hi, g_lo, g):
    span = 8 * FRAME
    start = pl.multiple_of(g * (2 * span), 2 * span)
    left = audio[:, pl.ds(start, span)].reshape(8 * OUTER, INNER)
    right = audio[:, pl.ds(start + span, span)].reshape(8 * OUTER, INNER)
    both = jnp.concatenate([left, right], axis=1)
    outer = outer.at[lax.rem(g, 2)]
    outer[...] = (dot(first_hi[...], both) + dot(first_lo[...], both)).reshape(outer.shape)
    frame = pl.multiple_of(g * GROUP, GROUP)

    def turned(k):
        re, im, c, s = outer[0, k], outer[1, k], twist[0, k], twist[1, k]
        return re * c + im * s, im * c - re * s

    def step(k, carry):
        before_re, before_im, re, im = carry
        after_re, after_im = turned(k + 1)
        out_re = re - 0.5 * (before_re + after_re)
        out_im = im - 0.5 * (before_im + after_im)
        value = jnp.concatenate(
            [
                jnp.concatenate([out_re[:, :INNER], out_im[:, :INNER]], axis=1),
                jnp.concatenate([out_re[:, INNER:], out_im[:, INNER:]], axis=1),
            ],
            axis=0,
        )
        hi = value.astype(B16)
        g_hi[k, pl.ds(frame, GROUP), :] = hi
        g_lo[k, pl.ds(frame, GROUP), :] = (value - hi.astype(F32)).astype(B16)
        return re, im, after_re, after_im

    zero_re, zero_im = turned(0)
    one_re, one_im = turned(1)
    lax.fori_loop(0, HALF_K + 1, step, (one_re, -one_im, zero_re, zero_im), unroll=True)


def second_stage(second_hi, second_lo, g_hi, g_lo, mag):
    def magnitudes(lhs_hi, lhs_lo, hi, lo):
        out = dot_t(lhs_hi, hi) + dot_t(lhs_hi, lo) + dot_t(lhs_lo, hi)
        half = out.shape[0] // 2
        re, im = out[:half], out[half:]
        return jnp.sqrt(re * re + im * im)

    def put(at, a, b):
        rows = jnp.concatenate([a.reshape(NF, 8, FRAMES), b.reshape(NF, 8, FRAMES)], axis=1)
        mag[:, pl.ds(pl.multiple_of(at * 8, 16), 16), :] = rows.astype(B16)

    def halves(ref):
        return jnp.concatenate([ref[0:64], ref[128:192]], axis=0)

    def pair(p):
        hi = g_hi[pl.ds(2 * p, 2)].reshape(2 * FRAMES, 2 * INNER)
        lo = g_lo[pl.ds(2 * p, 2)].reshape(2 * FRAMES, 2 * INNER)
        return magnitudes(second_hi[...], second_lo[...], hi, lo)

    middle = magnitudes(halves(second_hi), halves(second_lo), g_hi[HALF_K], g_lo[HALF_K])
    out = pair(0)
    put(0, out[:64, :FRAMES], out[:64, FRAMES:])
    put(HALF_K, middle, out[64:, FRAMES:])

    def step(p, _):
        out = pair(p)
        put(2 * p, out[:64, :FRAMES], out[:64, FRAMES:])
        put(HALF_K + 2 * p, out[64:, :FRAMES], out[64:, FRAMES:])
        return 0

    lax.fori_loop(1, HALF_K // 2, step, 0, unroll=True)


def kernel(
    audio_hbm, w_hbm, h_hbm, first_hi_hbm, first_lo_hbm, twist_hbm, second_hi_hbm, second_lo_hbm,
    place_hbm,
    w_out, h_out,
    audio, w_in, h_in, first_hi, first_lo, twist, second_hi, second_lo, place,
    outer, g_hi, g_lo, mag,
    start, gathered, comp, act,
    send_core, recv_core, send_plane, recv_plane, sums, last,
    gram_mine, gram_core, gram_z, gram_plane,
    audio_sem, load_sem, gather_sem, core_sems, plane_sem, z_sem, wide_sem, fwd_sem, last_sem, act_sem,
    gram_core_sem, gram_z_sem, gram_plane_sem,
):
    f, t = lax.axis_index("freq"), lax.axis_index("tm")
    y, c = lax.div(f, NC), lax.rem(f, NC)
    z, x = lax.div(t, NX), lax.rem(t, NX)
    far, m = lax.div(z, 2), lax.rem(z, 2)
    q = y * NX + x
    own_slot = 2 * q + m
    span = 16 * FRAME

    def signal(freq, tm):
        pl.semaphore_signal(
            pltpu.get_barrier_semaphore(), inc=1, device_id={"freq": freq, "tm": tm},
            device_id_type=MESH,
        )

    def remote(src, dst, sems, freq, tm):
        return pltpu.make_async_remote_copy(
            src_ref=src, dst_ref=dst, send_sem=sems.at[0], recv_sem=sems.at[1],
            device_id={"freq": freq, "tm": tm}, device_id_type=MESH,
        )

    def drain(ref, sem):
        pltpu.make_async_copy(ref, ref, sem).wait()

    def slot_device(slot):
        chip = lax.div(slot, 2)
        zz = z - m + lax.rem(slot, 2)
        return NC * lax.div(chip, NX) + c, NX * zz + lax.rem(chip, NX)

    def near_peer(i):
        return slot_device(lax.rem(own_slot + i, NS))

    def far_peer(i):
        return f, NX * (2 * lax.rem(far + i, NZ // 2) + m) + x

    def z_peer(i):
        return f, NX * lax.rem(z + i, NZ) + x

    def plane_peer(i):
        return slot_device(2 * lax.rem(q + i, NQ) + m)

    def load_audio(g):
        part = pl.ds(pl.multiple_of(g * span, span), span)
        return pltpu.make_async_copy(audio_hbm.at[:, part], audio.at[:, part], audio_sem.at[g])

    def load(src, dst, i):
        return pltpu.make_async_copy(src, dst, load_sem.at[i])

    loads = [
        load(src, dst, i)
        for i, (src, dst) in enumerate(
            (
                (first_hi_hbm, first_hi),
                (first_lo_hbm, first_lo),
                (twist_hbm, twist),
                (w_hbm, w_in),
                (place_hbm, place),
                (second_hi_hbm, second_hi),
                (second_lo_hbm, second_lo),
                (h_hbm, h_in),
            )
        )
    ]

    def each(low, high, body):
        def step(i, _):
            body(i)
            return 0

        lax.fori_loop(low, high, step, 0)

    load_audio(0).start()
    for copy in loads[:3]:
        copy.start()
    each(1, NZ // 2, lambda i: signal(*far_peer(i)))
    each(1, NZ // 2, lambda i: signal(f, NX * (2 * lax.rem(far + i, NZ // 2) + 1 - m) + x))
    each(1, NS, lambda i: signal(*near_peer(i)))
    each(0, NY, lambda i: signal(NC * i + (1 - c), t))
    each(1, GROUPS, lambda g: load_audio(g).start())
    for copy in loads[3:]:
        copy.start()
    for copy in loads[:3]:
        copy.wait()

    def spectra(p):
        for g in (2 * p, 2 * p + 1):
            load_audio(g).wait()
        for g in (2 * p, 2 * p + 1):
            first_stage(audio, first_hi, first_lo, twist, outer, g_hi, g_lo, g)

    each(0, EARLY // 2, spectra)

    for copy in loads[3:]:
        copy.wait()
    lane = lax.broadcasted_iota(jnp.int32, (COMP, 128), 1)
    low = lane < HALF
    mine = lax.div(lane, HALF) == m
    spread = dot(jnp.concatenate(terms(w_in[...]), axis=0), place[...])
    spread = spread[:COMP] + spread[COMP : 2 * COMP] + spread[2 * COMP :]
    gram = dot_t(spread, spread, HIGHEST)
    gram = pack(gram)
    hi = gram.astype(B16).astype(F32)
    start[f, NX * COMP :, :] = jnp.concatenate([hi, gram - hi], axis=0).astype(B16)
    for j in range(NX):
        block = spread[:, 128 * j : 128 * j + 128]
        last[2 * j] = block
        start[f, COMP * j : COMP * j + COMP, :] = block.astype(B16)
    comp[...] = last[2 * x]
    act[...] = h_in[:, pl.ds(pl.multiple_of(f * FRAMES, FRAMES), FRAMES)]

    pl.semaphore_wait(pltpu.get_barrier_semaphore(), (NS - 1) + 2 * (NZ // 2 - 1) + NY)

    def send_start(i):
        remote(start.at[f], start.at[f], gather_sem, lax.rem(f + i, NF), t).start()

    each(1, NF, send_start)
    each(EARLY // 2, GROUPS // 2, spectra)
    second_stage(second_hi, second_lo, g_hi, g_lo, mag)
    drain(start.at[pl.ds(0, NF - 1)], gather_sem.at[1])

    for it in range(ITERS):
        def product(core):
            total = jnp.zeros((COMP, FRAMES), F32)
            for yy in range(NY):
                if it == 0:
                    rows = [start[NC * yy + core, COMP * j : COMP * j + COMP, :] for j in range(NX)]
                else:
                    first = core * NS + 2 * NX * yy
                    rows = [
                        jnp.where(low, gathered[first + 2 * j], gathered[first + 2 * j + 1])
                        for j in range(NX)
                    ]
                total += dot(jnp.concatenate(rows, axis=1), mag[NC * yy + core])
            return total

        def gram_of(core):
            total = jnp.zeros((COMP, 128), F32)

            def add(i, total):
                at = core * NS + 2 * i
                return total + jnp.where(low, gathered[at + 1], gathered[at]).astype(F32)

            return lax.fori_loop(0, NQ, add, total, unroll=4)

        numer_h = product(c)
        gram_w = gram_of(c) if it > 0 else None
        if it == 1:
            drain(gathered.at[pl.ds(0, NS)], fwd_sem.at[1])
        numer_h += product(1 - c)
        if it == 0:
            total = start[0, NX * COMP :, :].astype(F32)
            for i in range(1, NF):
                total += start[i, NX * COMP :, :].astype(F32)
            gram_w = unpack(total[:8] + total[8:])
        else:
            gram_w += gram_of(1 - c)
            gram_w = (gram_w[:, :32] + gram_w[:, 64:96]) + (gram_w[:, 32:64] + gram_w[:, 96:])
        state = act[...]
        state = state * numer_h / dot(gram_w, state, HIGHEST)
        act[...] = state
        rounded = state.astype(B16)
        gram_mine[it] = pack(dot_t(state, state, HIGHEST))
        remote(
            gram_mine.at[it], gram_core.at[it], gram_core_sem.at[it], NC * y + (1 - c), t
        ).start()

        core_sem = core_sems.at[it]
        order = (2, 1, 3, 0)

        def partial(freq):
            return dot_t(rounded, mag[freq])

        for step, dy in enumerate(order):
            yy = lax.rem(y + dy, NY)
            value = partial(NC * yy + (1 - c))
            for j in range(NX):
                send_core[it, yy * NX + j] = value[:, 128 * j : 128 * j + 128]
            slots = pl.ds(yy * NX, NX)
            remote(
                send_core.at[it, slots], recv_core.at[it, slots], core_sem.at[step],
                NC * y + (1 - c), t,
            ).start()
        for step, dy in enumerate(order):
            yy = lax.rem(y + dy, NY)
            value = partial(NC * yy + c)
            drain(recv_core.at[it, pl.ds(yy * NX, NX)], core_sem.at[step, 1])
            for j in range(NX):
                chip = yy * NX + j
                tile = value[:, 128 * j : 128 * j + 128] + recv_core[it, chip]
                top, bottom = tile[:PACKED], tile[PACKED:]
                send_plane[it, 2 * chip] = jnp.where(low[:PACKED], top, swap(bottom))
                send_plane[it, 2 * chip + 1] = jnp.where(low[:PACKED], swap(top), bottom)
            for dx in range(NX):
                xx = lax.rem(x + dx, NX)
                for dm in range(2):
                    slot = 2 * (yy * NX + xx) + lax.rem(m + dm, 2)
                    if dy == 0 and dx == 0 and dm == 0:
                        recv_plane[it, own_slot] = send_plane[it, own_slot]
                    else:
                        remote(
                            send_plane.at[it, slot], recv_plane.at[it, own_slot],
                            plane_sem.at[it], *slot_device(slot),
                        ).start()

        drain(gram_core.at[it], gram_core_sem.at[it, 1])
        gram_z[it, z] = gram_mine[it] + gram_core[it]

        def gram_to_z(i):
            own = gram_z.at[it, z]
            remote(own, own, gram_z_sem.at[it], *z_peer(i)).start()

        each(1, NZ, gram_to_z)

        drain(recv_plane.at[it, pl.ds(0, NS - 1)], plane_sem.at[it, 1])
        total = recv_plane[it, 0]
        for i in range(1, NS):
            total += recv_plane[it, i]
        sums[it, far] = total

        def share(i):
            own = sums.at[it, far]
            remote(own, own, z_sem.at[it], *far_peer(i)).start()

        each(1, NZ // 2, share)
        drain(gram_z.at[it, pl.ds(0, NZ - 1)], gram_z_sem.at[it, 1])
        gram_h = gram_z[it, 0]
        for i in range(1, NZ):
            gram_h += gram_z[it, i]
        gram_plane[it, q] = gram_h

        def gram_to_plane(i):
            own = gram_plane.at[it, q]
            remote(own, own, gram_plane_sem.at[it], *plane_peer(i)).start()

        each(1, NQ, gram_to_plane)
        if it == ITERS - 1:
            columns = pl.ds(pl.multiple_of(f * FRAMES, FRAMES), FRAMES)
            h_out[:, columns] = state

            def send_act(i):
                remote(act, h_out.at[:, columns], act_sem, lax.rem(f + i, NF), t).start()

            each(1, NF, send_act)

        drain(sums.at[it, pl.ds(0, NZ // 2 - 1)], z_sem.at[it, 1])
        total = sums[it, 0]
        for i in range(1, NZ // 2):
            total += sums[it, i]
        drain(gram_plane.at[it, pl.ds(0, NQ - 1)], gram_plane_sem.at[it, 1])
        gram_h = gram_plane[it, 0]
        for i in range(1, NQ):
            gram_h += gram_plane[it, i]
        packed = total
        other = swap(packed)
        numer_w = jnp.concatenate(
            [jnp.where(m == 0, packed, other), jnp.where(m == 0, other, packed)], axis=0
        )
        own = comp[...]
        below = dot(unpack(gram_h), own, HIGHEST)
        own = jnp.where(mine, own * numer_w / jnp.where(mine, below, 1.0), 0.0)
        comp[...] = own

        if it < ITERS - 1:
            at = c * NS + own_slot
            gathered[at] = gather_slot(mine, own, dot_t(own, own, HIGHEST))

            def spread_near(i):
                slot = gathered.at[at]
                remote(slot, slot, wide_sem, *near_peer(i)).start()

            each(1, NS, spread_near)
            drain(gathered.at[pl.ds(0, NS - 1)], wide_sem.at[1])
            slots = gathered.at[pl.ds(c * NS, NS)]
            remote(slots, slots, fwd_sem, NC * y + (1 - c), t).start()
        else:
            end = 2 * x + m
            last[end] = own

            def spread_x(i):
                peer = lax.rem(end + i, 2 * NX)
                zz = z - m + lax.rem(peer, 2)
                remote(comp, last.at[end], last_sem, f, NX * zz + lax.div(peer, 2)).start()

            each(1, 2 * NX, spread_x)
            drain(last.at[pl.ds(0, 2 * NX - 1)], last_sem.at[1])

    whole = [jnp.where(low, last[2 * j], last[2 * j + 1]) for j in range(NX)]
    whole = jnp.concatenate(whole, axis=1)
    whole = dot_t(jnp.concatenate(terms(whole), axis=0), place[...])
    w_out[...] = whole[:COMP] + whole[COMP : 2 * COMP] + whole[2 * COMP :]

    drain(h_out.at[:, pl.ds(0, (NF - 1) * FRAMES)], act_sem.at[1])
    drain(h_out.at[:, pl.ds(0, (NF - 1) * FRAMES)], act_sem.at[0])
    drain(start.at[pl.ds(0, NF - 1)], gather_sem.at[0])
    drain(gathered.at[pl.ds(0, NS - 1)], wide_sem.at[0])
    drain(gathered.at[pl.ds(0, NS)], fwd_sem.at[0])
    drain(last.at[pl.ds(0, 2 * NX - 1)], last_sem.at[0])
    for it in range(ITERS):
        for step in range(NY):
            drain(send_core.at[it, pl.ds(0, NX)], core_sems.at[it, step, 0])
        drain(send_plane.at[it, pl.ds(0, NS - 1)], plane_sem.at[it, 0])
        drain(sums.at[it, pl.ds(0, NZ // 2 - 1)], z_sem.at[it, 0])
        drain(gram_mine.at[it], gram_core_sem.at[it, 0])
        drain(gram_z.at[it, pl.ds(0, NZ - 1)], gram_z_sem.at[it, 0])
        drain(gram_plane.at[it, pl.ds(0, NQ - 1)], gram_plane_sem.at[it, 0])


def deliver(w_ref, h_ref, w_out, h_out, w_held, h_held, sem):
    into = (
        pltpu.make_async_copy(w_ref, w_held, sem.at[0]),
        pltpu.make_async_copy(h_ref, h_held, sem.at[1]),
    )
    out = (
        pltpu.make_async_copy(w_held, w_out, sem.at[2]),
        pltpu.make_async_copy(h_held, h_out, sem.at[3]),
    )
    for copy in into:
        copy.start()
    for load, store in zip(into, out):
        load.wait()
        store.start()
    for store in out:
        store.wait()


def shards(audio, w_start, h_start):
    vmem = pl.BlockSpec(memory_space=pltpu.VMEM)
    dma = pltpu.SemaphoreType.DMA
    constants = [jnp.asarray(table) for table in tables()]
    operands = (audio, w_start, h_start, *constants)
    hbm = pl.BlockSpec(memory_space=pltpu.HBM)
    shapes = (
        jax.ShapeDtypeStruct((COMP, OWN), F32),
        jax.ShapeDtypeStruct((COMP, NF * FRAMES), F32),
    )
    results = pl.pallas_call(
        kernel,
        out_shape=shapes,
        in_specs=[hbm] * len(operands),
        out_specs=(vmem, vmem),
        scratch_shapes=[
            *(pltpu.VMEM(operand.shape, operand.dtype) for operand in operands),
            pltpu.VMEM((2, 2, NK, 8, 2 * INNER), F32),
            pltpu.VMEM((HALF_K + 1, FRAMES, 2 * INNER), B16),
            pltpu.VMEM((HALF_K + 1, FRAMES, 2 * INNER), B16),
            pltpu.VMEM((NF, OWN, FRAMES), B16),
            pltpu.VMEM((NF, START, 128), B16),
            pltpu.VMEM((NC * NS, COMP, 128), B16),
            pltpu.VMEM((COMP, 128), F32),
            pltpu.VMEM((COMP, FRAMES), F32),
            pltpu.VMEM((ITERS, NQ, COMP, 128), F32),
            pltpu.VMEM((ITERS, NQ, COMP, 128), F32),
            pltpu.VMEM((ITERS, NS, PACKED, 128), F32),
            pltpu.VMEM((ITERS, NS, PACKED, 128), F32),
            pltpu.VMEM((ITERS, NZ // 2, PACKED, 128), F32),
            pltpu.VMEM((2 * NX, COMP, 128), F32),
            pltpu.VMEM((ITERS, 8, 128), F32),
            pltpu.VMEM((ITERS, 8, 128), F32),
            pltpu.VMEM((ITERS, NZ, 8, 128), F32),
            pltpu.VMEM((ITERS, NQ, 8, 128), F32),
            dma((GROUPS,)),
            dma((8,)),
            dma((2,)),
            dma((ITERS, NY, 2)),
            dma((ITERS, 2)),
            dma((ITERS, 2)),
            dma((2,)),
            dma((2,)),
            dma((2,)),
            dma((2,)),
            dma((ITERS, 2)),
            dma((ITERS, 2)),
            dma((ITERS, 2)),
        ],
        compiler_params=pltpu.CompilerParams(
            collective_id=0, has_side_effects=True, vmem_limit_bytes=64 * 2**20 - 2**16
        ),
    )(*operands)
    return pl.pallas_call(
        deliver,
        out_shape=shapes,
        in_specs=[hbm] * 2,
        out_specs=(hbm, hbm),
        scratch_shapes=[*(pltpu.VMEM(shape.shape, F32) for shape in shapes), dma((4,))],
        compiler_params=pltpu.CompilerParams(vmem_limit_bytes=64 * 2**20 - 2**16),
    )(*results)


def solution(mesh):
    placed = (P("tm", "freq"), P(None, "freq"), P(None, "tm"))
    return jax.shard_map(
        shards,
        mesh=mesh,
        in_specs=placed,
        out_specs=(P(None, "freq"), P(None, "tm")),
        check_vma=False,
    )
```
